32 devices in a mesh: ctx: 8 (over z, x), wsh: 4 (over y, core).
Axes of the slice: x: 2, y: 2, z: 4, core: 2. Of those that a mesh axis runs over, the one named last changes fastest.
Arguments:
- inputs: bfloat16 [2048, 8, 576], P('ctx', 'wsh'), may hold values from -6 to 6
- query_weight: bfloat16 [576, 576], P('wsh'), may hold values from -0.5 to 0.5
- key_weight: bfloat16 [576, 192], P('wsh'), may hold values from -0.25 to 0.25
- value_weight: bfloat16 [576, 192], P('wsh'), may hold values from -0.25 to 0.25
- output_weight: bfloat16 [576, 576], P('wsh'), may hold values from -1.5 to 1.5
- gate_weight: bfloat16 [576, 1536], P('wsh'), may hold values from -0.25 to 0.25
- up_weight: bfloat16 [576, 1536], P('wsh'), may hold values from -0.25 to 0.25
- down_weight: bfloat16 [1536, 576], P('wsh'), may hold values from -0.15625 to 0.15625
- attn_gain: bfloat16 [576], P('wsh'), may hold values from 0.5 to 1.5
- ffn_gain: bfloat16 [576], P('wsh'), may hold values from 0.5 to 1.5
- cotangent: bfloat16 [2048, 8, 576], P('ctx', 'wsh'), may hold values from -6 to 6
Outputs:
- layer_out: bfloat16 [2048, 8, 576], P('ctx', 'wsh')
- input_grad: bfloat16 [2048, 8, 576], P('ctx', 'wsh')
- query_grad: float32 [576, 576], P('wsh')
- key_grad: float32 [576, 192], P('wsh')
- value_grad: float32 [576, 192], P('wsh')
- project_grad: float32 [576, 576], P('wsh')
- gate_grad: float32 [576, 1536], P('wsh')
- up_grad: float32 [576, 1536], P('wsh')
- down_grad: float32 [1536, 576], P('wsh')
- attn_gain_grad: float32 [576], P('wsh')
- ffn_gain_grad: float32 [576], P('wsh')
The draws below stay inside these ranges and needn't reach their ends.
All inputs are finite; a program needn't handle non-finite values.
Results may differ from the reference program's by a relative error of at most 0.017.
The reference program's roundings to bfloat16 on the way count: a program that leaves them out, or rounds other values in their place, can miss the bound.
Values may be sent and summed in bfloat16 or wider, within the bound.
A program may use at most 256 MiB of HBM per device.

```python
import math
import jax
import jax.numpy as jnp
from jax import lax

D = 576
HEADS = 9
KV_HEADS = 3
HEAD = 64
FF = 1536
LENGTH = 2048
SEQS = 8


def block_scale(rng, dims, cuts, least, top_value):
    loudness = 1.0
    for dim, blocks in cuts:
        draws = jax.random.uniform(jax.random.fold_in(jax.random.fold_in(rng, 6), dim), (blocks,), jnp.float32, least / len(cuts), top_value / len(cuts))
        loudness = loudness * jnp.repeat(jnp.exp(draws), dims[dim] // blocks).reshape((-1,) + (1,) * (len(dims) - 1 - dim))
    return loudness


def centred(key, dims, deviation, reach, split=(), kind=jnp.bfloat16):
    level = block_scale(key, dims, split, -0.22, 0.18) if split else 1.0
    array = jax.random.normal(key, dims, jnp.float32) * deviation * level
    return jnp.minimum(jnp.maximum(array, -reach), reach).astype(kind)


def setup_inputs(seed: int = 0) -> dict:
    arg_keys = jax.random.split(jax.random.key(seed), 12)
    return {
        "inputs": centred(arg_keys[0], (LENGTH, SEQS, D), 1.0, 6.0, ((0, 8), (1, 4))),
        "query_weight": centred(arg_keys[1], (D, D), (D // 4) ** -0.5, 0.5, ((0, 4),)),
        "key_weight": centred(arg_keys[2], (D, KV_HEADS * HEAD), D ** -0.5, 0.25, ((0, 4),)),
        "value_weight": centred(arg_keys[3], (D, KV_HEADS * HEAD), D ** -0.5, 0.25, ((0, 4),)),
        "output_weight": centred(arg_keys[4], (D, D), (max(1, D * 64 // LENGTH)) ** -0.5, 1.5, ((0, 4),)),
        "gate_weight": centred(arg_keys[5], (D, FF), D ** -0.5, 0.25, ((0, 4),)),
        "up_weight": centred(arg_keys[6], (D, FF), D ** -0.5, 0.25, ((0, 4),)),
        "down_weight": centred(arg_keys[7], (FF, D), FF ** -0.5, 0.15625, ((0, 4),)),
        "attn_gain": jnp.clip(1.0 + 0.1 * jax.random.normal(arg_keys[8], (D,), jnp.float32), 0.5, 1.5).astype(jnp.bfloat16),
        "ffn_gain": jnp.clip(1.0 + 0.1 * jax.random.normal(arg_keys[9], (D,), jnp.float32), 0.5, 1.5).astype(jnp.bfloat16),
        "cotangent": centred(arg_keys[10], (LENGTH, SEQS, D), 1.0, 6.0, ((0, 8), (1, 4))),
    }


epsilon = 1e-05
rope_base = 100000.0
highest = lax.Precision.HIGHEST

@jax.custom_vjp
def low(v):
    return lax.optimization_barrier(v.astype(jnp.bfloat16)).astype(jnp.float32)

@jax.custom_vjp
def low_back(v):
    return v

def low_keep(v):
    return (low(v), None)

def low_pass(kept, grad):
    return (grad,)

def back_keep(v):
    return (v, None)

def back_low(kept, grad):
    return (low(grad),)
low.defvjp(low_keep, low_pass)
low_back.defvjp(back_keep, back_low)

def product(left, right):
    return jnp.dot(left, right, precision=highest, preferred_element_type=jnp.float32)

def rms_norm(values, gain):
    factor = lax.rsqrt(lax.optimization_barrier(jnp.mean(values * values, axis=-1, keepdims=True)) + epsilon)
    return values * factor * gain

def rope_tables(positions):
    half = HEAD // 2
    rates = rope_base ** (-(2.0 * jnp.arange(half, dtype=jnp.float32)) / HEAD)
    angles = positions[:, None] * rates[None, :]
    return (jnp.cos(angles), jnp.sin(angles))

def rotate(values, cosine, sine):
    half = values.shape[-1] // 2
    first = values[..., :half]
    second = values[..., half:]
    cosine = cosine[:, None, :]
    sine = sine[:, None, :]
    return jnp.concatenate([first * cosine - second * sine, second * cosine + first * sine], axis=-1)

def attention(queries, keys, values):
    length = queries.shape[0]
    width = math.gcd(length, 1024)
    count = length // width
    per_group = HEADS // KV_HEADS
    scale = HEAD ** (-0.5)
    grouped = queries.reshape(count, width, KV_HEADS, per_group, HEAD)
    starts = jnp.arange(count, dtype=jnp.int32) * width
    key_pos = jnp.arange(length, dtype=jnp.int32)

    def block(item):
        part, start = item
        scores = low_back(jnp.einsum('qgrd,kgd->grqk', part, keys, precision=highest) * scale)
        query_pos = start + jnp.arange(width, dtype=jnp.int32)
        causal = query_pos[:, None] >= key_pos[None, :]
        powers = jnp.where(causal, jnp.exp(scores), 0.0)
        total = lax.optimization_barrier(jnp.sum(powers, axis=-1))
        weighted = low_back(jnp.einsum('grqk,kgd->qgrd', low(powers), values, precision=highest))
        return weighted / jnp.transpose(total, (2, 0, 1))[..., None]
    mixed = lax.map(jax.checkpoint(block), (grouped, starts))
    return mixed.reshape(length, HEADS * HEAD)

def layer(inputs, w_query, w_key, w_value, w_out, w_gate, w_up, w_down, gain_one, gain_two):
    length = inputs.shape[0]
    normed = low(rms_norm(inputs, gain_one))
    queries = low_back(product(normed, w_query)).reshape(length, HEADS, HEAD)
    keys = low_back(product(normed, w_key)).reshape(length, KV_HEADS, HEAD)
    values = low(low_back(product(normed, w_value))).reshape(length, KV_HEADS, HEAD)
    cosine, sine = rope_tables(jnp.arange(length, dtype=jnp.float32))
    queries = low(rotate(queries, cosine, sine))
    keys = low(rotate(keys, cosine, sine))
    mixed = low(attention(queries, keys, values))
    middle = inputs + low_back(product(mixed, w_out))
    normed_two = low(rms_norm(middle, gain_two))
    gate = low_back(product(normed_two, w_gate))
    up = low_back(product(normed_two, w_up))
    hidden = low(jax.nn.silu(gate) * up)
    return middle + low_back(product(hidden, w_down))

def reference(inputs, query_weight, key_weight, value_weight, output_weight, gate_weight, up_weight, down_weight, attn_gain, ffn_gain, cotangent):
    params = (query_weight.astype(jnp.float32), key_weight.astype(jnp.float32), value_weight.astype(jnp.float32), output_weight.astype(jnp.float32), gate_weight.astype(jnp.float32), up_weight.astype(jnp.float32), down_weight.astype(jnp.float32), attn_gain.astype(jnp.float32), ffn_gain.astype(jnp.float32))
    sequences = jnp.transpose(inputs.astype(jnp.float32), (1, 0, 2))
    seeds = jnp.transpose(cotangent.astype(jnp.float32), (1, 0, 2))
    group = math.gcd(SEQS, max(1, 4096 // LENGTH))

    def forward(values, w_query, w_key, w_value, w_out, w_gate, w_up, w_down, gain_one, gain_two):
        blocks = values.reshape(SEQS // group, group, LENGTH, D)

        def run(block):
            return jax.vmap(lambda single: layer(single, w_query, w_key, w_value, w_out, w_gate, w_up, w_down, gain_one, gain_two))(block)
        return lax.map(jax.checkpoint(run), blocks).reshape(SEQS, LENGTH, D)
    result, pullback = jax.vjp(forward, sequences, params[0], params[1], params[2], params[3], params[4], params[5], params[6], params[7], params[8])
    grads = pullback(seeds)
    layer_out = jnp.transpose(result, (1, 0, 2)).astype(jnp.bfloat16)
    input_grad = jnp.transpose(grads[0], (1, 0, 2)).astype(jnp.bfloat16)
    return (layer_out, input_grad, grads[1], grads[2], grads[3], grads[4], grads[5], grads[6], grads[7], grads[8], grads[9])
```

```python
import math

import jax
import jax.numpy as jnp
from jax import lax
from jax.sharding import PartitionSpec as P

D = 576
HEADS = 9
KV_HEADS = 3
HEAD = 64


epsilon = 1e-05
rope_base = 100000.0


def rms_norm(values, gain):
    factor = lax.rsqrt(jnp.mean(values * values, axis=-1, keepdims=True) + epsilon)
    return values * factor * gain


def rope_tables(positions):
    half = HEAD // 2
    rates = rope_base ** (-(2.0 * jnp.arange(half, dtype=jnp.float32)) / HEAD)
    angles = positions[:, None] * rates[None, :]
    return (jnp.cos(angles), jnp.sin(angles))


def rotate(values, cosine, sine):
    half = values.shape[-1] // 2
    first = values[..., :half]
    second = values[..., half:]
    cosine = cosine[:, None, :]
    sine = sine[:, None, :]
    return jnp.concatenate(
        [first * cosine - second * sine, second * cosine + first * sine], axis=-1
    )


def sweep(state, pairs, last_query, step):
    length = pairs.shape[0]
    width = math.gcd(length, 1024)
    count = length // width
    upper = jnp.clip(last_query // width + 1, 0, count)

    def advance(index, carry):
        begin = index * width
        piece = lax.dynamic_slice_in_dim(pairs, begin, width, 0)
        return step(carry, piece, begin)

    return lax.fori_loop(0, upper, advance, state)


def local(
    inputs,
    query_weight,
    key_weight,
    value_weight,
    output_weight,
    gate_weight,
    up_weight,
    down_weight,
    attn_gain,
    ffn_gain,
    cotangent,
):
    first_pack = jnp.concatenate(
        [query_weight, key_weight, value_weight, attn_gain[:, None], ffn_gain[:, None]], axis=1
    )
    first_all = lax.all_gather(first_pack, "wsh", axis=0, tiled=True)
    w_first = first_all[:, : D + 2 * KV_HEADS * HEAD]
    gain_first = first_all[:, D + 2 * KV_HEADS * HEAD]
    gain_second = first_all[:, D + 2 * KV_HEADS * HEAD + 1]
    width = gate_weight.shape[1]
    middle_pack = jnp.concatenate([output_weight, gate_weight, up_weight], axis=1)
    middle_pack, down_weight, first_all = lax.optimization_barrier(
        (middle_pack, down_weight, first_all)
    )
    middle_all = lax.all_gather(middle_pack, "wsh", axis=0, tiled=True)
    w_down = lax.all_gather(down_weight, "wsh", axis=0, tiled=True)
    w_out = middle_all[:, :D]
    w_gate_up = middle_all[:, D:]
    gain_first = gain_first.astype(jnp.float32)
    gain_second = gain_second.astype(jnp.float32)
    tokens = inputs.shape[0]
    batch = inputs.shape[1]
    rows = tokens * batch
    per_group = HEADS // KV_HEADS
    pair_width = KV_HEADS * HEAD
    scale = HEAD ** (-0.5)
    cycle_index = lax.axis_index("ctx")
    cycle_size = lax.axis_size("ctx")
    start_pos = cycle_index * tokens
    last_query = start_pos + tokens - 1
    query_pos = start_pos + jnp.arange(tokens, dtype=jnp.int32)
    cosine, sine = rope_tables(query_pos.astype(jnp.float32))
    full_length = cycle_size * tokens
    residual = inputs.reshape(rows, D).astype(jnp.float32)
    normed = rms_norm(residual, gain_first).astype(jnp.bfloat16)
    first_pre = jnp.dot(normed, w_first, preferred_element_type=jnp.float32)
    query_pre = first_pre[:, :D]
    key_pre = first_pre[:, D : D + pair_width]
    value_pre = first_pre[:, D + pair_width :]
    queries = (
        rotate(query_pre.reshape(tokens, batch * HEADS, HEAD), cosine, sine)
        .astype(jnp.bfloat16)
        .reshape(tokens, batch, KV_HEADS, per_group, HEAD)
    )
    keys = (
        rotate(key_pre.reshape(tokens, batch * KV_HEADS, HEAD), cosine, sine)
        .astype(jnp.bfloat16)
        .reshape(tokens, batch, pair_width)
    )
    pairs = jnp.concatenate(
        [keys, value_pre.astype(jnp.bfloat16).reshape(tokens, batch, pair_width)], axis=-1
    )

    def split_pairs(piece):
        count = piece.shape[0]
        return (
            piece[..., :pair_width].reshape(count, batch, KV_HEADS, HEAD),
            piece[..., pair_width:].reshape(count, batch, KV_HEADS, HEAD),
        )

    def exponents(piece_keys, first):
        scores = (
            jnp.einsum("qsgrd,ksgd->sgrqk", queries, piece_keys, preferred_element_type=jnp.float32)
            * scale
        )
        key_pos = first + jnp.arange(piece_keys.shape[0], dtype=jnp.int32)
        causal = query_pos[:, None] >= key_pos[None, :]
        return jnp.where(causal, jnp.exp(scores), 0.0)

    def forward_step(state, piece, first):
        weighted, total = state
        piece_keys, piece_values = split_pairs(piece)
        powers = exponents(piece_keys, first)
        weighted = weighted + jnp.einsum(
            "sgrqk,ksgd->qsgrd",
            powers.astype(jnp.bfloat16),
            piece_values,
            preferred_element_type=jnp.float32,
        )
        return (weighted, total + jnp.sum(powers, axis=-1))

    all_pairs = lax.all_gather(pairs, "ctx", axis=0, tiled=True)
    start_state = (
        jnp.zeros((tokens, batch, KV_HEADS, per_group, HEAD), jnp.float32),
        jnp.zeros((batch, KV_HEADS, per_group, tokens), jnp.float32),
    )
    weighted, total = sweep(
        start_state, all_pairs, last_query, forward_step
    )
    totals_moved = jnp.transpose(total, (3, 0, 1, 2))[..., None]
    mixed = weighted / totals_moved
    mixed_low = mixed.astype(jnp.bfloat16).reshape(rows, D)
    middle = residual + jnp.dot(mixed_low, w_out, preferred_element_type=jnp.float32)
    normed_two = rms_norm(middle, gain_second).astype(jnp.bfloat16)
    gate_up = jnp.dot(normed_two, w_gate_up, preferred_element_type=jnp.float32)
    gate = gate_up[:, :width]
    up = gate_up[:, width:]
    hidden = (jax.nn.silu(gate) * up).astype(jnp.bfloat16)
    result = middle + jnp.dot(hidden, w_down, preferred_element_type=jnp.float32)
    layer_out = result.astype(jnp.bfloat16).reshape(tokens, batch, D)
    seed = cotangent.reshape(rows, D)
    grad_down = jnp.einsum("nf,nd->fd", hidden, seed, preferred_element_type=jnp.float32)
    grad_hidden = jnp.einsum("nd,fd->nf", seed, w_down, preferred_element_type=jnp.float32)
    unused_value, swiglu_back = jax.vjp(lambda left, right: jax.nn.silu(left) * right, gate, up)
    grad_gate_f, grad_up_f = swiglu_back(grad_hidden)
    back = jnp.concatenate(
        [grad_gate_f.astype(jnp.bfloat16), grad_up_f.astype(jnp.bfloat16)], axis=1
    )
    grad_gate_up = jnp.einsum("nd,nf->df", normed_two, back, preferred_element_type=jnp.float32)
    grad_normed_two = jnp.einsum("nf,df->nd", back, w_gate_up, preferred_element_type=jnp.float32)
    unused_norm, second_norm_back = jax.vjp(rms_norm, middle, gain_second)
    grad_middle_norm, grad_gain_second = second_norm_back(grad_normed_two)
    grad_middle = seed.astype(jnp.float32) + grad_middle_norm
    attn_seed = grad_middle.astype(jnp.bfloat16)
    grad_project = jnp.einsum("nd,ne->de", mixed_low, attn_seed, preferred_element_type=jnp.float32)
    grad_mixed = jnp.einsum(
        "ne,de->nd", attn_seed, w_out, preferred_element_type=jnp.float32
    ).reshape(tokens, batch, KV_HEADS, per_group, HEAD)
    scaled = (grad_mixed / totals_moved).astype(jnp.bfloat16)
    offset = jnp.sum(grad_mixed * mixed, axis=-1) / totals_moved[..., 0]
    middle_grads = jnp.concatenate([grad_project, grad_gate_up], axis=1).astype(jnp.bfloat16)
    down_grads = grad_down.astype(jnp.bfloat16)
    middle_grads, down_grads, scaled, offset = lax.optimization_barrier(
        (middle_grads, down_grads, scaled, offset)
    )
    down_share = lax.psum_scatter(down_grads, "wsh", scatter_dimension=0, tiled=True)
    middle_share = lax.psum_scatter(middle_grads, "wsh", scatter_dimension=0, tiled=True)
    offset_moved = jnp.transpose(offset, (1, 2, 3, 0))[..., None]

    def backward_step(state, piece, first):
        grad_queries, grad_pairs = state
        piece_keys, piece_values = split_pairs(piece)
        powers = exponents(piece_keys, first)
        inner = jnp.einsum(
            "qsgrd,ksgd->sgrqk", scaled, piece_values, preferred_element_type=jnp.float32
        )
        grad_scores = (powers * (inner - offset_moved)).astype(jnp.bfloat16)
        grad_queries = (
            grad_queries
            + jnp.einsum(
                "sgrqk,ksgd->qsgrd", grad_scores, piece_keys, preferred_element_type=jnp.float32
            )
            * scale
        )
        grad_keys = (
            jnp.einsum(
                "sgrqk,qsgrd->ksgd", grad_scores, queries, preferred_element_type=jnp.float32
            )
            * scale
        )
        grad_values = jnp.einsum(
            "sgrqk,qsgrd->ksgd",
            powers.astype(jnp.bfloat16),
            scaled,
            preferred_element_type=jnp.float32,
        )
        count = piece.shape[0]
        term = jnp.concatenate(
            [
                grad_keys.reshape(count, batch, pair_width),
                grad_values.reshape(count, batch, pair_width),
            ],
            axis=-1,
        )
        return (grad_queries, lax.dynamic_update_slice_in_dim(grad_pairs, term, first, 0))

    back_state = (
        jnp.zeros((tokens, batch, KV_HEADS, per_group, HEAD), jnp.float32),
        jnp.zeros((full_length, batch, 2 * pair_width), jnp.float32),
    )
    grad_queries, grad_pairs = sweep(
        back_state, all_pairs, last_query, backward_step
    )
    own_pairs = lax.psum_scatter(
        grad_pairs.astype(jnp.bfloat16), "ctx", scatter_dimension=0, tiled=True
    ).astype(jnp.float32)
    query_back = (
        rotate(grad_queries.reshape(tokens, batch * HEADS, HEAD), cosine, -sine)
        .astype(jnp.bfloat16)
        .reshape(rows, D)
    )
    key_back = (
        rotate(own_pairs[..., :pair_width].reshape(tokens, batch * KV_HEADS, HEAD), cosine, -sine)
        .astype(jnp.bfloat16)
        .reshape(rows, pair_width)
    )
    value_back = own_pairs[..., pair_width:].astype(jnp.bfloat16).reshape(rows, pair_width)
    first_back = jnp.concatenate([query_back, key_back, value_back], axis=1)
    grad_first = jnp.einsum("nd,nk->dk", normed, first_back, preferred_element_type=jnp.float32)
    grad_normed = jnp.einsum("nk,dk->nd", first_back, w_first, preferred_element_type=jnp.float32)
    unused_first, first_norm_back = jax.vjp(rms_norm, residual, gain_first)
    grad_residual, grad_gain_first = first_norm_back(grad_normed)
    input_grad = (grad_middle + grad_residual).astype(jnp.bfloat16).reshape(tokens, batch, D)
    first_grads = jnp.concatenate(
        [grad_first, grad_gain_first[:, None], grad_gain_second[:, None]], axis=1
    ).astype(jnp.bfloat16)
    first_share = lax.psum_scatter(first_grads, "wsh", scatter_dimension=0, tiled=True)
    down_own = lax.psum(down_share, "ctx").astype(jnp.float32)
    middle_own = lax.psum(middle_share, "ctx").astype(jnp.float32)
    first_own = lax.psum(first_share, "ctx").astype(jnp.float32)
    return (
        layer_out,
        input_grad,
        first_own[:, :D],
        first_own[:, D : D + pair_width],
        first_own[:, D + pair_width : D + 2 * pair_width],
        middle_own[:, :D],
        middle_own[:, D : D + width],
        middle_own[:, D + width :],
        down_own,
        first_own[:, D + 2 * pair_width],
        first_own[:, D + 2 * pair_width + 1],
    )


def solution(mesh):
    in_specs = (
        P("ctx", "wsh", None),
        P("wsh", None),
        P("wsh", None),
        P("wsh", None),
        P("wsh", None),
        P("wsh", None),
        P("wsh", None),
        P("wsh", None),
        P("wsh"),
        P("wsh"),
        P("ctx", "wsh", None),
    )
    out_specs = (
        P("ctx", "wsh", None),
        P("ctx", "wsh", None),
        P("wsh", None),
        P("wsh", None),
        P("wsh", None),
        P("wsh", None),
        P("wsh", None),
        P("wsh", None),
        P("wsh", None),
        P("wsh"),
        P("wsh"),
    )
    return jax.shard_map(local, mesh=mesh, in_specs=in_specs, out_specs=out_specs, check_vma=False)
```

```python
import functools
import math

import jax
import jax.numpy as jnp
from jax import lax
from jax.experimental import pallas as pl
from jax.experimental.pallas import tpu as pltpu
from jax.sharding import PartitionSpec as P

D = 576
HEADS = 9
KV_HEADS = 3
HEAD = 64


epsilon = 1e-05
rope_base = 100000.0


def rms_norm(values, gain):
    factor = lax.rsqrt(jnp.mean(values * values, axis=-1, keepdims=True) + epsilon)
    return values * factor * gain


def rope_tables(positions):
    half = HEAD // 2
    rates = rope_base ** (-(2.0 * jnp.arange(half, dtype=jnp.float32)) / HEAD)
    angles = positions[:, None] * rates[None, :]
    return (jnp.cos(angles), jnp.sin(angles))


def rotate(values, cosine, sine):
    half = values.shape[-1] // 2
    first = values[..., :half]
    second = values[..., half:]
    cosine = cosine[:, None, :]
    sine = sine[:, None, :]
    return jnp.concatenate(
        [first * cosine - second * sine, second * cosine + first * sine], axis=-1
    )


def sweep(state, pairs, last_query, step):
    length = pairs.shape[0]
    width = math.gcd(length, 1024)
    count = length // width
    upper = jnp.clip(last_query // width + 1, 0, count)

    def advance(index, carry):
        begin = index * width
        piece = lax.dynamic_slice_in_dim(pairs, begin, width, 0)
        return step(carry, piece, begin)

    return lax.fori_loop(0, upper, advance, state)


COPIES = 10


def part_of(ref, rows, cols, by_cols, begin, count, pieces):
    if by_cols:
        size = cols // pieces
        return ref.at[:, pl.ds(pl.multiple_of(begin * size, 128), count * size)]
    size = rows // pieces
    return ref.at[pl.ds(pl.multiple_of(begin * size, 16), count * size), :]


def add_into(out_ref, terms, rows):
    @pl.loop(0, rows // 16)
    def _(index):
        at = pl.ds(pl.multiple_of(index * 16, 16), 16)
        total = terms[0][at, :].astype(jnp.float32)
        for term in terms[1:]:
            total = total + term[at, :].astype(jnp.float32)
        out_ref[at, :] = total.astype(out_ref.dtype)


def reduce_kernel(shapes, *refs):
    n = len(shapes)
    ins, outs = refs[:n], refs[n : 2 * n]
    scratch = refs[2 * n : 2 * n + 8 * n]
    send_sem, recv_sem = refs[2 * n + 8 * n :]
    wsh = lax.axis_index("wsh")
    ctx = lax.axis_index("ctx")
    high, low = wsh // 2, wsh % 2
    far, near = ctx // 2, ctx % 2
    pair_low = {"ctx": ctx, "wsh": high * 2 + (1 - low)}
    pair_high = {"ctx": ctx, "wsh": (1 - high) * 2 + low}
    pair_near = {"ctx": far * 2 + (1 - near), "wsh": wsh}
    others = [(far + 1 + k) % 4 for k in range(3)]
    pair_far = [{"ctx": other * 2 + near, "wsh": wsh} for other in others]

    barrier = pltpu.get_barrier_semaphore()
    for device in [pair_low, pair_high, pair_near] + pair_far:
        pl.semaphore_signal(barrier, inc=1, device_id=device, device_id_type=pl.DeviceIdType.MESH)
    pl.semaphore_wait(barrier, 6)

    started = {}

    def send(chunk, index, source, target, device):
        copy = pltpu.make_async_remote_copy(
            src_ref=source,
            dst_ref=target,
            send_sem=send_sem.at[chunk, index],
            recv_sem=recv_sem.at[chunk, index],
            device_id=device,
            device_id_type=pl.DeviceIdType.MESH,
        )
        copy.start()
        started[chunk, index] = copy

    def step(stage, chunk):
        rows, cols, by_cols = shapes[chunk]
        term, out = ins[chunk], outs[chunk]
        got_low, sum_low, got_high, sum_high, got_near, sum_near, got_far, full = scratch[
            8 * chunk : 8 * chunk + 8
        ]
        half_rows = rows if by_cols else rows // 2
        half_cols = cols // 2 if by_cols else cols
        piece_rows = rows if by_cols else rows // 8

        def half(ref, which):
            return part_of(ref, rows, cols, by_cols, which * 4, 4, 8)

        def piece(ref, which):
            return part_of(ref, rows, cols, by_cols, near * 4 + which, 1, 8)

        def quarter(ref, which):
            return part_of(ref, half_rows, half_cols, by_cols, which, 1, 4)

        if stage == 0:
            send(chunk, 0, term.at[:, 1 - low], got_low, pair_low)
        elif stage == 1:
            started[chunk, 0].wait_recv()
            for index in range(2):
                add_into(sum_low.at[index], [term.at[index, low], got_low.at[index]], rows)
            send(chunk, 1, sum_low.at[1 - high], got_high, pair_high)
        elif stage == 2:
            started[chunk, 1].wait_recv()
            add_into(sum_high, [sum_low.at[high], got_high], rows)
            send(chunk, 2, half(sum_high, 1 - near), got_near, pair_near)
        elif stage == 3:
            started[chunk, 2].wait_recv()
            add_into(sum_near, [half(sum_high, near), got_near], half_rows)
            for k in range(3):
                send(chunk, 3 + k, quarter(sum_near, others[k]), got_far.at[k], pair_far[k])
        elif stage == 4:
            for k in range(3):
                started[chunk, 3 + k].wait_recv()
            add_into(
                piece(full, far),
                [quarter(sum_near, far)] + [got_far.at[k] for k in range(3)],
                piece_rows,
            )
            for k in range(3):
                send(chunk, 6 + k, piece(full, far), piece(full, far), pair_far[k])
        elif stage == 5:
            for k in range(3):
                started[chunk, 6 + k].wait_recv()
            send(chunk, 9, half(full, near), half(full, near), pair_near)
        else:
            started[chunk, 9].wait_recv()
            add_into(out, [full], rows)

    for turn in range(n + 6):
        for stage in range(6, -1, -1):
            chunk = turn - stage
            if 0 <= chunk < n:
                step(stage, chunk)
    for copy in started.values():
        copy.wait_send()


def reduce_all(terms, by_cols, collective_id):
    shapes = tuple((term.shape[1], term.shape[2], cut) for term, cut in zip(terms, by_cols))
    scratch = []
    size = 0
    for rows, cols, cut in shapes:
        half_shape = (rows, cols // 2) if cut else (rows // 2, cols)
        piece_shape = (rows, cols // 8) if cut else (rows // 8, cols)
        for shape in (
            (2, rows, cols),
            (2, rows, cols),
            (rows, cols),
            (rows, cols),
            half_shape,
            half_shape,
            (3,) + piece_shape,
            (rows, cols),
        ):
            scratch.append(pltpu.VMEM(shape, jnp.bfloat16))
        size += rows * cols * 2
    count = len(shapes)
    return pl.pallas_call(
        functools.partial(reduce_kernel, shapes),
        out_shape=[jax.ShapeDtypeStruct((rows, cols), jnp.float32) for rows, cols, _ in shapes],
        in_specs=[pl.BlockSpec(memory_space=pltpu.VMEM)] * count,
        out_specs=[pl.BlockSpec(memory_space=pltpu.VMEM)] * count,
        scratch_shapes=scratch
        + [pltpu.SemaphoreType.DMA((count, COPIES)), pltpu.SemaphoreType.DMA((count, COPIES))],
        compiler_params=pltpu.CompilerParams(
            collective_id=collective_id, has_side_effects=True, vmem_limit_bytes=48 * 1024 * 1024
        ),
        cost_estimate=pl.CostEstimate(
            flops=size * 8, bytes_accessed=size * 100, transcendentals=0
        ),
    )(*[term.reshape(2, 2, *term.shape[1:]) for term in terms])


def local(
    inputs,
    query_weight,
    key_weight,
    value_weight,
    output_weight,
    gate_weight,
    up_weight,
    down_weight,
    attn_gain,
    ffn_gain,
    cotangent,
):
    first_pack = jnp.concatenate(
        [query_weight, key_weight, value_weight, attn_gain[:, None], ffn_gain[:, None]], axis=1
    )
    first_all = lax.all_gather(first_pack, "wsh", axis=0, tiled=True)
    w_first = first_all[:, : D + 2 * KV_HEADS * HEAD]
    gain_first = first_all[:, D + 2 * KV_HEADS * HEAD]
    gain_second = first_all[:, D + 2 * KV_HEADS * HEAD + 1]
    width = gate_weight.shape[1]
    middle_pack = jnp.concatenate([output_weight, gate_weight, up_weight], axis=1)
    middle_pack, down_weight, first_all = lax.optimization_barrier(
        (middle_pack, down_weight, first_all)
    )
    middle_all = lax.all_gather(middle_pack, "wsh", axis=0, tiled=True)
    w_down = lax.all_gather(down_weight, "wsh", axis=0, tiled=True)
    w_out = middle_all[:, :D]
    w_gate_up = middle_all[:, D:]
    gain_first = gain_first.astype(jnp.float32)
    gain_second = gain_second.astype(jnp.float32)
    tokens = inputs.shape[0]
    batch = inputs.shape[1]
    rows = tokens * batch
    per_group = HEADS // KV_HEADS
    pair_width = KV_HEADS * HEAD
    scale = HEAD ** (-0.5)
    cycle_index = lax.axis_index("ctx")
    cycle_size = lax.axis_size("ctx")
    start_pos = cycle_index * tokens
    last_query = start_pos + tokens - 1
    query_pos = start_pos + jnp.arange(tokens, dtype=jnp.int32)
    cosine, sine = rope_tables(query_pos.astype(jnp.float32))
    full_length = cycle_size * tokens
    residual = inputs.reshape(rows, D).astype(jnp.float32)
    normed = rms_norm(residual, gain_first).astype(jnp.bfloat16)
    first_pre = jnp.dot(normed, w_first, preferred_element_type=jnp.float32)
    query_pre = first_pre[:, :D]
    key_pre = first_pre[:, D : D + pair_width]
    value_pre = first_pre[:, D + pair_width :]
    queries = (
        rotate(query_pre.reshape(tokens, batch * HEADS, HEAD), cosine, sine)
        .astype(jnp.bfloat16)
        .reshape(tokens, batch, KV_HEADS, per_group, HEAD)
    )
    keys = (
        rotate(key_pre.reshape(tokens, batch * KV_HEADS, HEAD), cosine, sine)
        .astype(jnp.bfloat16)
        .reshape(tokens, batch, pair_width)
    )
    pairs = jnp.concatenate(
        [keys, value_pre.astype(jnp.bfloat16).reshape(tokens, batch, pair_width)], axis=-1
    )

    def split_pairs(piece):
        count = piece.shape[0]
        return (
            piece[..., :pair_width].reshape(count, batch, KV_HEADS, HEAD),
            piece[..., pair_width:].reshape(count, batch, KV_HEADS, HEAD),
        )

    def exponents(piece_keys, first):
        scores = (
            jnp.einsum("qsgrd,ksgd->sgrqk", queries, piece_keys, preferred_element_type=jnp.float32)
            * scale
        )
        key_pos = first + jnp.arange(piece_keys.shape[0], dtype=jnp.int32)
        causal = query_pos[:, None] >= key_pos[None, :]
        return jnp.where(causal, jnp.exp(scores), 0.0)

    def forward_step(state, piece, first):
        weighted, total = state
        piece_keys, piece_values = split_pairs(piece)
        powers = exponents(piece_keys, first)
        weighted = weighted + jnp.einsum(
            "sgrqk,ksgd->qsgrd",
            powers.astype(jnp.bfloat16),
            piece_values,
            preferred_element_type=jnp.float32,
        )
        return (weighted, total + jnp.sum(powers, axis=-1))

    all_pairs = lax.all_gather(pairs, "ctx", axis=0, tiled=True)
    start_state = (
        jnp.zeros((tokens, batch, KV_HEADS, per_group, HEAD), jnp.float32),
        jnp.zeros((batch, KV_HEADS, per_group, tokens), jnp.float32),
    )
    weighted, total = sweep(
        start_state, all_pairs, last_query, forward_step
    )
    totals_moved = jnp.transpose(total, (3, 0, 1, 2))[..., None]
    mixed = weighted / totals_moved
    mixed_low = mixed.astype(jnp.bfloat16).reshape(rows, D)
    middle = residual + jnp.dot(mixed_low, w_out, preferred_element_type=jnp.float32)
    normed_two = rms_norm(middle, gain_second).astype(jnp.bfloat16)
    gate_up = jnp.dot(normed_two, w_gate_up, preferred_element_type=jnp.float32)
    gate = gate_up[:, :width]
    up = gate_up[:, width:]
    hidden = (jax.nn.silu(gate) * up).astype(jnp.bfloat16)
    result = middle + jnp.dot(hidden, w_down, preferred_element_type=jnp.float32)
    layer_out = result.astype(jnp.bfloat16).reshape(tokens, batch, D)
    seed = cotangent.reshape(rows, D)
    grad_down = jnp.einsum("nf,nd->fd", hidden, seed, preferred_element_type=jnp.float32)
    grad_hidden = jnp.einsum("nd,fd->nf", seed, w_down, preferred_element_type=jnp.float32)
    unused_value, swiglu_back = jax.vjp(lambda left, right: jax.nn.silu(left) * right, gate, up)
    grad_gate_f, grad_up_f = swiglu_back(grad_hidden)
    back = jnp.concatenate(
        [grad_gate_f.astype(jnp.bfloat16), grad_up_f.astype(jnp.bfloat16)], axis=1
    )
    grad_gate_up = jnp.einsum("nd,nf->df", normed_two, back, preferred_element_type=jnp.float32)
    grad_normed_two = jnp.einsum("nf,df->nd", back, w_gate_up, preferred_element_type=jnp.float32)
    unused_norm, second_norm_back = jax.vjp(rms_norm, middle, gain_second)
    grad_middle_norm, grad_gain_second = second_norm_back(grad_normed_two)
    grad_middle = seed.astype(jnp.float32) + grad_middle_norm
    attn_seed = grad_middle.astype(jnp.bfloat16)
    grad_project = jnp.einsum("nd,ne->de", mixed_low, attn_seed, preferred_element_type=jnp.float32)
    grad_mixed = jnp.einsum(
        "ne,de->nd", attn_seed, w_out, preferred_element_type=jnp.float32
    ).reshape(tokens, batch, KV_HEADS, per_group, HEAD)
    scaled = (grad_mixed / totals_moved).astype(jnp.bfloat16)
    offset = jnp.sum(grad_mixed * mixed, axis=-1) / totals_moved[..., 0]
    direct = cycle_size == 8 and lax.axis_size("wsh") == 4
    owners = lax.axis_size("wsh")
    if direct:
        spare = -(D + 2 * width) % 1024
        middle_grads = jnp.concatenate(
            [grad_gate_up, grad_project, jnp.zeros((D, spare), jnp.float32)], axis=1
        ).astype(jnp.bfloat16)
        middle_terms = [
            middle_grads[:, at : at + 1024].reshape(owners, D // owners, 1024)
            for at in range(0, middle_grads.shape[1], 1024)
        ]
        down_term = grad_down.astype(jnp.bfloat16).reshape(owners, width // owners, D)
    else:
        middle_grads = jnp.concatenate([grad_gate_up, grad_project], axis=1).astype(jnp.bfloat16)
        down_grads = grad_down.astype(jnp.bfloat16)
        middle_share = lax.psum_scatter(middle_grads, "wsh", scatter_dimension=0, tiled=True)
        down_share = lax.psum_scatter(down_grads, "wsh", scatter_dimension=0, tiled=True)
    offset_moved = jnp.transpose(offset, (1, 2, 3, 0))[..., None]

    def backward_step(state, piece, first):
        grad_queries, grad_pairs = state
        piece_keys, piece_values = split_pairs(piece)
        powers = exponents(piece_keys, first)
        inner = jnp.einsum(
            "qsgrd,ksgd->sgrqk", scaled, piece_values, preferred_element_type=jnp.float32
        )
        grad_scores = (powers * (inner - offset_moved)).astype(jnp.bfloat16)
        grad_queries = (
            grad_queries
            + jnp.einsum(
                "sgrqk,ksgd->qsgrd", grad_scores, piece_keys, preferred_element_type=jnp.float32
            )
            * scale
        )
        grad_keys = (
            jnp.einsum(
                "sgrqk,qsgrd->ksgd", grad_scores, queries, preferred_element_type=jnp.float32
            )
            * scale
        )
        grad_values = jnp.einsum(
            "sgrqk,qsgrd->ksgd",
            powers.astype(jnp.bfloat16),
            scaled,
            preferred_element_type=jnp.float32,
        )
        count = piece.shape[0]
        term = jnp.concatenate(
            [
                grad_keys.reshape(count, batch, pair_width),
                grad_values.reshape(count, batch, pair_width),
            ],
            axis=-1,
        )
        return (grad_queries, lax.dynamic_update_slice_in_dim(grad_pairs, term, first, 0))

    back_state = (
        jnp.zeros((tokens, batch, KV_HEADS, per_group, HEAD), jnp.float32),
        jnp.zeros((full_length, batch, 2 * pair_width), jnp.float32),
    )
    grad_queries, grad_pairs = sweep(
        back_state, all_pairs, last_query, backward_step
    )
    own_pairs = lax.psum_scatter(
        grad_pairs.astype(jnp.bfloat16), "ctx", scatter_dimension=0, tiled=True
    ).astype(jnp.float32)
    query_back = (
        rotate(grad_queries.reshape(tokens, batch * HEADS, HEAD), cosine, -sine)
        .astype(jnp.bfloat16)
        .reshape(rows, D)
    )
    key_back = (
        rotate(own_pairs[..., :pair_width].reshape(tokens, batch * KV_HEADS, HEAD), cosine, -sine)
        .astype(jnp.bfloat16)
        .reshape(rows, pair_width)
    )
    value_back = own_pairs[..., pair_width:].astype(jnp.bfloat16).reshape(rows, pair_width)
    first_back = jnp.concatenate([query_back, key_back, value_back], axis=1)
    grad_first = jnp.einsum("nd,nk->dk", normed, first_back, preferred_element_type=jnp.float32)
    grad_normed = jnp.einsum("nk,dk->nd", first_back, w_first, preferred_element_type=jnp.float32)
    unused_first, first_norm_back = jax.vjp(rms_norm, residual, gain_first)
    grad_residual, grad_gain_first = first_norm_back(grad_normed)
    input_grad = (grad_middle + grad_residual).astype(jnp.bfloat16).reshape(tokens, batch, D)
    first_grads = [grad_first, grad_gain_first[:, None], grad_gain_second[:, None]]
    if direct:
        spare = -(D + 2 * pair_width + 2) % 1024
        first_grads.append(jnp.zeros((D, spare), jnp.float32))
    first_grads = jnp.concatenate(first_grads, axis=1).astype(jnp.bfloat16)
    if direct:
        count = len(middle_terms)
        sums = reduce_all(middle_terms + [down_term], [True] * count + [False], 1)
        middle_own = jnp.concatenate(sums[:count], axis=1)
        down_own = sums[count]
        first_own = reduce_all(
            [first_grads.reshape(owners, D // owners, first_grads.shape[1])], [True], 2
        )[0]
    else:
        first_share = lax.psum_scatter(first_grads, "wsh", scatter_dimension=0, tiled=True)
        down_own = lax.psum(down_share, "ctx").astype(jnp.float32)
        middle_own = lax.psum(middle_share, "ctx").astype(jnp.float32)
        first_own = lax.psum(first_share, "ctx").astype(jnp.float32)
    return (
        layer_out,
        input_grad,
        first_own[:, :D],
        first_own[:, D : D + pair_width],
        first_own[:, D + pair_width : D + 2 * pair_width],
        middle_own[:, 2 * width : 2 * width + D],
        middle_own[:, :width],
        middle_own[:, width : 2 * width],
        down_own,
        first_own[:, D + 2 * pair_width],
        first_own[:, D + 2 * pair_width + 1],
    )


def solution(mesh):
    in_specs = (
        P("ctx", "wsh", None),
        P("wsh", None),
        P("wsh", None),
        P("wsh", None),
        P("wsh", None),
        P("wsh", None),
        P("wsh", None),
        P("wsh", None),
        P("wsh"),
        P("wsh"),
        P("ctx", "wsh", None),
    )
    out_specs = (
        P("ctx", "wsh", None),
        P("ctx", "wsh", None),
        P("wsh", None),
        P("wsh", None),
        P("wsh", None),
        P("wsh", None),
        P("wsh", None),
        P("wsh", None),
        P("wsh", None),
        P("wsh"),
        P("wsh"),
    )
    return jax.shard_map(local, mesh=mesh, in_specs=in_specs, out_specs=out_specs, check_vma=False)
```
